256 devices in a mesh: rows: 32 (over z, y), cols: 8 (over x, core).
Axes of the slice: x: 4, y: 4, z: 8, core: 2. Of those that a mesh axis runs over, the one named last changes fastest.
Arguments:
- embedding: float32 [40960, 4096], P('rows', 'cols'), may hold values from -50 to 50
- test_matrix: float32 [4096, 640], P('cols'), may hold values from -0.09375 to 0.09375
Outputs:
- whitened: float32 [40960, 640], P(('rows', 'cols'))
- col_basis: float32 [4096, 640], P('cols')
The draws below stay inside these ranges and needn't reach their ends.
All inputs are finite; a program needn't handle non-finite values.
Results may differ from the reference program's by a relative error of at most 0.000092.
Values sent between devices are 32-bit elements; how exact they have to be, the bound alone decides.
A program may use at most 64 MiB of HBM per device.

```python
import math
import jax
import jax.numpy as jnp
from jax import lax

N = 4096
K = 640
M = 40960


def draw_embedding(key, part):
    key = jax.random.fold_in(key, 11)
    entry_key, row_key, col_key = jax.random.split(key, 3)
    entries = jnp.clip(jax.random.normal(entry_key, (M, N), jnp.float32), -5.0, 5.0)
    spread = 0.5
    row_scale = jnp.exp(math.log(10.0) * jax.random.uniform(row_key, (M, 1), jnp.float32, -spread, spread))
    col_scale = jnp.exp(math.log(10.0) * jax.random.uniform(col_key, (1, N), jnp.float32, -0.5, 0.5))
    return (entries * row_scale * col_scale).astype(jnp.float32)


def block_scale(own_key, dims, cuts, least, top_value):
    level, own = 1.0, jax.random.fold_in(own_key, 6)
    for position, blocks in cuts:
        draws = jnp.exp(jax.random.uniform(jax.random.fold_in(own, position), (blocks,), jnp.float32, least / len(cuts), top_value / len(cuts)))
        level = level * jnp.repeat(draws, dims[position] // blocks).reshape([-1 if axis == position else 1 for axis in range(len(dims))])
    return level


def scatter_about(rng, dims, deviation, limit, pieces=(), held_as=jnp.bfloat16):
    factor_of = block_scale(rng, dims, pieces, -0.22, 0.18) if pieces else 1.0
    values = jax.random.normal(rng, dims, jnp.float32) * deviation * factor_of
    return jnp.minimum(jnp.maximum(values, -limit), limit).astype(held_as)


def setup_inputs(seed: int = 0) -> dict:
    key_of = jax.random.split(jax.random.key(seed), 3)
    return {
        "embedding": draw_embedding(jax.random.fold_in(key_of[2], 71), 0),
        "test_matrix": scatter_about(key_of[1], (N, K), N ** -0.5, 0.09375, ((0, 8),), jnp.float32),
    }


precise = lax.Precision.HIGHEST

def contract(left_mat, right_mat):
    return lax.dot_general(left_mat.astype(jnp.float32), right_mat.astype(jnp.float32), (((0,), (0,)), ((), ())), precision=precise, preferred_element_type=jnp.float32)

def orthonormal(matrix):
    gram_full = contract(matrix, matrix) / matrix.shape[0]
    lower_factor = jnp.linalg.cholesky(gram_full)
    return jax.scipy.linalg.solve_triangular(lower_factor, matrix.T, lower=True).T

def reference(embedding, test_matrix):
    sketch = jnp.dot(embedding.astype(jnp.float32), test_matrix.astype(jnp.float32), precision=precise, preferred_element_type=jnp.float32)
    whitened = orthonormal(sketch)
    dual_full = contract(embedding, whitened)
    col_basis = orthonormal(dual_full)
    return (whitened, col_basis)
```

```python
import jax
import jax.numpy as jnp
from jax import lax
from jax.experimental import pallas as pl
from jax.experimental.pallas import tpu as pltpu
from jax.sharding import PartitionSpec as P

precise = lax.Precision.HIGHEST
BLOCK = 128
TILE = 8
TILES = BLOCK // TILE


def dot(left_mat, right_mat, left_dim, right_dim):
    return lax.dot_general(
        left_mat,
        right_mat,
        (((left_dim,), (right_dim,)), ((), ())),
        precision=precise,
        preferred_element_type=jnp.float32,
    )


def invert_factor(rows):
    shape = (TILE, BLOCK)
    lane = lax.broadcasted_iota(jnp.int32, shape, 1)
    sub = lax.broadcasted_iota(jnp.int32, shape, 0)
    rows = list(rows)
    inverse = [
        jnp.where(lane == sub + TILE * i, 1.0, 0.0).astype(jnp.float32) for i in range(TILES)
    ]
    for tile in range(TILES):
        spread = {
            i: [
                jnp.broadcast_to(rows[i][:, col : col + 1], shape)
                for col in range(tile * TILE, tile * TILE + TILE)
            ]
            for i in range(tile, TILES)
        }
        pivots = None
        for t in range(TILE):
            pivot = jnp.broadcast_to(spread[tile][t][t : t + 1, :], shape)
            pivots = pivot if pivots is None else jnp.where(sub == t, pivot, pivots)
            inv_pivot = 1.0 / pivot
            pivot_cols = [
                jnp.broadcast_to(spread[tile][u][t : t + 1, :], shape) for u in range(t + 1, TILE)
            ]
            pivot_row = jnp.broadcast_to(rows[tile][t : t + 1, :], shape)
            pivot_inv = jnp.broadcast_to(inverse[tile][t : t + 1, :], shape)
            for i in range(tile, TILES):
                factor = spread[i][t] * inv_pivot
                if i == tile:
                    factor = jnp.where(sub > t, factor, 0.0)
                for u in range(t + 1, TILE):
                    spread[i][u] = spread[i][u] - factor * pivot_cols[u - t - 1]
                rows[i] = rows[i] - factor * pivot_row
                inverse[i] = inverse[i] - factor * pivot_inv
        inverse[tile] = inverse[tile] * lax.rsqrt(pivots)
    return jnp.concatenate(inverse, 0)


def whiten_kernel(gram_ref, mat_ref, out_ref, gram, mat):
    count = gram_ref.shape[0] // BLOCK
    gram[...] = gram_ref[...]
    mat[...] = mat_ref[...]
    for k in range(count):
        lo, hi = k * BLOCK, (k + 1) * BLOCK
        inverse = invert_factor([gram[lo + TILE * i : lo + TILE * (i + 1), lo:hi] for i in range(TILES)])
        done = dot(mat[:, lo:hi], inverse, 1, 1)
        out_ref[:, lo:hi] = done
        if k + 1 < count:
            below = dot(gram[hi:, lo:hi], inverse, 1, 1)
            gram[hi:, hi:] = gram[hi:, hi:] - dot(below, below, 1, 1)
            mat[:, hi:] = mat[:, hi:] - dot(done, below, 1, 1)


def whiten(matrix, gram_full):
    return pl.pallas_call(
        whiten_kernel,
        out_shape=jax.ShapeDtypeStruct(matrix.shape, jnp.float32),
        scratch_shapes=[
            pltpu.VMEM(gram_full.shape, jnp.float32),
            pltpu.VMEM(matrix.shape, jnp.float32),
        ],
        compiler_params=pltpu.CompilerParams(vmem_limit_bytes=40 * 2**20),
    )(gram_full, matrix)


def body(embedding, test_matrix):
    rows_local, width_local = embedding.shape
    col_count = lax.axis_size("cols")
    row_count = lax.axis_size("rows")
    share_rows = rows_local // col_count
    total_rows = rows_local * row_count
    total_width = width_local * col_count
    sketch = lax.psum(dot(embedding, test_matrix, 1, 0), "cols")
    gram_full = lax.psum(dot(sketch, sketch, 0, 0), "rows") / total_rows
    projected = lax.psum(dot(embedding, sketch, 0, 0), "rows")
    share = lax.dynamic_slice_in_dim(sketch, lax.axis_index("cols") * share_rows, share_rows, 0)
    both = whiten(jnp.concatenate([share, projected], 0), gram_full)
    whitened, dual_full = both[:share_rows], both[share_rows:]
    dual_gram = lax.psum(dot(dual_full, dual_full, 0, 0), "cols") / total_width
    return whitened, whiten(dual_full, dual_gram)


def solution(mesh):
    placed = (P("rows", "cols"), P("cols", None))
    return jax.shard_map(
        body,
        mesh=mesh,
        in_specs=placed,
        out_specs=(P(("rows", "cols"), None), P("cols", None)),
        check_vma=False,
    )
```

```python
import functools

import jax
import jax.numpy as jnp
from jax import lax
from jax.experimental import pallas as pl
from jax.experimental.pallas import tpu as pltpu
from jax.sharding import PartitionSpec as P

precise = lax.Precision.HIGHEST
BLOCK = 128
TILE = 8
TILES = BLOCK // TILE


def dot(left_mat, right_mat, left_dim, right_dim):
    return lax.dot_general(
        left_mat,
        right_mat,
        (((left_dim,), (right_dim,)), ((), ())),
        precision=precise,
        preferred_element_type=jnp.float32,
    )


def invert_factor(rows):
    shape = (TILE, BLOCK)
    lane = lax.broadcasted_iota(jnp.int32, shape, 1)
    sub = lax.broadcasted_iota(jnp.int32, shape, 0)
    rows = list(rows)
    inverse = [
        jnp.where(lane == sub + TILE * i, 1.0, 0.0).astype(jnp.float32) for i in range(TILES)
    ]
    for tile in range(TILES):
        spread = {
            i: [
                jnp.broadcast_to(rows[i][:, col : col + 1], shape)
                for col in range(tile * TILE, tile * TILE + TILE)
            ]
            for i in range(tile, TILES)
        }
        pivots = None
        for t in range(TILE):
            pivot = jnp.broadcast_to(spread[tile][t][t : t + 1, :], shape)
            pivots = pivot if pivots is None else jnp.where(sub == t, pivot, pivots)
            inv_pivot = 1.0 / pivot
            pivot_cols = [
                jnp.broadcast_to(spread[tile][u][t : t + 1, :], shape) for u in range(t + 1, TILE)
            ]
            pivot_row = jnp.broadcast_to(rows[tile][t : t + 1, :], shape)
            pivot_inv = jnp.broadcast_to(inverse[tile][t : t + 1, :], shape)
            for i in range(tile, TILES):
                factor = spread[i][t] * inv_pivot
                if i == tile:
                    factor = jnp.where(sub > t, factor, 0.0)
                for u in range(t + 1, TILE):
                    spread[i][u] = spread[i][u] - factor * pivot_cols[u - t - 1]
                rows[i] = rows[i] - factor * pivot_row
                inverse[i] = inverse[i] - factor * pivot_inv
        inverse[tile] = inverse[tile] * lax.rsqrt(pivots)
    return jnp.concatenate(inverse, 0)


XS, YS, ZS = 4, 4, 8
VMEM_LIMIT = 56 * 2**20


def device(z, y, x, k):
    return {"rows": z * YS + y, "cols": x * 2 + k}


def place():
    r, c = lax.axis_index("rows"), lax.axis_index("cols")
    return r // YS, r % YS, c // 2, c % 2


def along(axis, here, d):
    z, y, x, k = here
    if axis == "z":
        return device((z + d) % ZS, y, x, k)
    if axis == "y":
        return device(z, (y + d) % YS, x, k)
    if axis == "x":
        return device(z, y, (x + d) % XS, k)
    return device(z, y, x, 1 - k)


SIZE = {"z": ZS, "y": YS, "x": XS, "k": 2}


def enter(axes, here):
    barrier = pltpu.get_barrier_semaphore()
    count = 0
    for axis in axes:
        for d in range(1, SIZE[axis]):
            pl.semaphore_signal(
                barrier, inc=1, device_id=along(axis, here, d), device_id_type=pl.DeviceIdType.MESH
            )
            count += 1
    return barrier, count


def send(src, dst, sems, slot, to):
    copy = pltpu.make_async_remote_copy(
        src_ref=src,
        dst_ref=dst,
        send_sem=sems.at[0, slot],
        recv_sem=sems.at[1, slot],
        device_id=to,
        device_id_type=pl.DeviceIdType.MESH,
    )
    copy.start()
    return copy


def scatter(axis, here, src, rows, landing, sems):
    pos = here["zyxk".index(axis)]
    return [
        send(
            src.at[pl.ds(((pos + d) % SIZE[axis]) * rows, rows)],
            landing.at[d - 1],
            sems,
            d - 1,
            along(axis, here, d),
        )
        for d in range(1, SIZE[axis])
    ]


def gather(axis, here, buf, first, rows, sems):
    return [
        send(
            buf.at[pl.ds(first, rows)], buf.at[pl.ds(first, rows)], sems, d - 1, along(axis, here, d)
        )
        for d in range(1, SIZE[axis])
    ]


def wait(copies):
    for copy in copies:
        copy.wait()


def total(first, landing):
    value = first
    for d in range(landing.shape[0]):
        value = value + landing[d]
    return value


def slots_of(mat, out):
    for i in range(5):
        lo = i * BLOCK
        strip = dot(mat[:, lo : lo + BLOCK], mat[:, : lo + BLOCK], 0, 0)
        for j in range(i + 1):
            slot = i * (i + 1) // 2 + j
            out[slot // 8, pl.ds((slot % 8) * BLOCK, BLOCK), :] = strip[:, j * BLOCK : (j + 1) * BLOCK]
    out[1, pl.ds(7 * BLOCK, BLOCK), :] = jnp.zeros((BLOCK, BLOCK), jnp.float32)


def sum_gram(here, part, sums, landings, sems, out):
    z, y, x, k = here
    by_k, by_y, by_z, by_x = landings
    sum_y, sum_z = sums
    rows_y, rows_z = 1024 // YS, 1024 // YS // ZS
    copy = send(part.at[1 - k], by_k, sems["k"], 0, along("k", here, 1))
    yield
    copy.wait()
    part[k] = part[k] + by_k[...]
    copies = scatter("y", here, part.at[k], rows_y, by_y, sems["y"])
    yield
    wait(copies)
    sum_y[...] = total(part[k, pl.ds(y * rows_y, rows_y), :], by_y)
    copies = scatter("z", here, sum_y, rows_z, by_z, sems["z"])
    yield
    wait(copies)
    by_x[x] = total(sum_y[pl.ds(z * rows_z, rows_z), :], by_z)
    copies = [
        send(by_x.at[x], by_x.at[x], sems["x"], d - 1, along("x", here, d)) for d in range(1, XS)
    ]
    yield
    wait(copies)
    first = y * rows_y + z * rows_z
    out[k, pl.ds(first, rows_z), :] = (by_x[0] + by_x[1]) + (by_x[2] + by_x[3])
    copies = gather("z", here, out.at[k], first, rows_z, sems["gz"])
    yield
    wait(copies)
    copies = gather("y", here, out.at[k], y * rows_y, rows_y, sems["gy"])
    yield
    wait(copies)
    copy = send(out.at[k], out.at[k], sems["gk"], 0, along("k", here, 1))
    yield
    copy.wait()


def sum_rows(here, order, part, sum_first, landings, sems, out):
    at = {"z": here[0], "y": here[1]}
    first, second = order
    rows_first = part.shape[0] // SIZE[first]
    rows_second = rows_first // SIZE[second]
    copies = scatter(first, here, part, rows_first, landings[0], sems[0])
    yield
    wait(copies)
    sum_first[...] = total(part[pl.ds(at[first] * rows_first, rows_first), :], landings[0])
    copies = scatter(second, here, sum_first, rows_second, landings[1], sems[1])
    yield
    wait(copies)
    mine = at[first] * rows_first + at[second] * rows_second
    out[pl.ds(mine, rows_second), :] = total(
        sum_first[pl.ds(at[second] * rows_second, rows_second), :], landings[1]
    )
    copies = gather(second, here, out, mine, rows_second, sems[2])
    yield
    wait(copies)
    copies = gather(first, here, out, at[first] * rows_first, rows_first, sems[3])
    yield
    wait(copies)


def sketch_kernel(
    emb_hbm, test_hbm,
    share_ref, proj_a_ref, proj_b_ref, gram_ref,
    emb, test, load_sems,
    part, by_core, by_x, core_sems, x_sems,
    slab, gx_sems, gcore_sems,
    proj_a, proj_b,
    a_sum, a_in0, a_in1, a_s0, a_s1, a_s2, a_s3,
    b_sum, b_in0, b_in1, b_s0, b_s1, b_s2, b_s3,
    gram_part, sum_y, sum_z, g_k, g_y, g_z, g_x, gs_k, gs_y, gs_z, gs_x, gs_gz, gs_gy, gs_gk,
):
    here = place()
    z, y, x, k = here
    me = x * 2 + k
    share = part.shape[2]
    barrier, count = enter("kxyz", here)
    load_test = pltpu.make_async_copy(test_hbm, test, load_sems.at[0])
    load_emb = pltpu.make_async_copy(emb_hbm, emb, load_sems.at[1])
    load_test.start()
    load_emb.start()
    load_test.wait()
    load_emb.wait()

    order = (2, 1, 3, 0)
    core_copies, x_copies = [], []

    def hand_on(step):
        core_copies[step].wait()
        part[step, k] = part[step, k] + by_core[step]
        d = order[step]
        if d:
            x_copies.append(send(part.at[step, k], by_x.at[d - 1], x_sems, d - 1, along("x", here, d)))

    for step, d in enumerate(order):
        target = (x + d) % XS

        @pl.loop(0, 2)
        def _(half):
            first = pl.multiple_of((target * 2 + half) * share, share)
            part[step, half] = dot(emb[pl.ds(first, share), :], test[...], 1, 0)

        if step == 0:
            pl.semaphore_wait(barrier, count)
        core_copies.append(
            send(part.at[step, 1 - k], by_core.at[step], core_sems, step, along("k", here, 1))
        )
        if step:
            hand_on(step - 1)
    hand_on(3)
    wait(x_copies)
    slab[me] = total(part[3, k], by_x)

    x_gather = {
        d: send(slab.at[me], slab.at[me], gx_sems, d - 1, along("x", here, d)) for d in (2, 1, 3)
    }
    core_gather = {0: send(slab.at[me], slab.at[me], gcore_sems, 0, along("k", here, 1))}
    share_ref[...] = slab[me]

    slots_of(share_ref, gram_part)
    gram_sum = sum_gram(
        here, gram_part, (sum_y, sum_z), (g_k, g_y, g_z, g_x),
        dict(k=gs_k, y=gs_y, z=gs_z, x=gs_x, gz=gs_gz, gy=gs_gy, gk=gs_gk), gram_ref,
    )
    next(gram_sum, None)

    def project(d):
        source = (x + XS - d) % XS
        core_gather[d].wait()
        for half in range(2):
            one = slab.at[source * 2 + half]
            rows = emb[pl.ds(pl.multiple_of((source * 2 + half) * share, share), share), :]
            for into, lo, hi in ((proj_a, 0, 384), (proj_b, 384, 640)):
                value = dot(rows, one[:, lo:hi], 0, 0)
                if d == 0 and half == 0:
                    into[...] = value
                else:
                    into[...] = into[...] + value

    def forward(d):
        x_gather[d].wait()
        source = (x + XS - d) % XS
        core_gather[d] = send(
            slab.at[source * 2 + k], slab.at[source * 2 + k], gcore_sems, d, along("k", here, 1)
        )

    next(gram_sum, None)
    project(0)
    forward(1)
    next(gram_sum, None)
    project(1)
    forward(3)
    project(3)
    next(gram_sum, None)
    forward(2)
    project(2)
    sum_a = sum_rows(here, "yz", proj_a, a_sum, (a_in0, a_in1), (a_s0, a_s1, a_s2, a_s3), proj_a_ref)
    sum_b = sum_rows(here, "zy", proj_b, b_sum, (b_in0, b_in1), (b_s0, b_s1, b_s2, b_s3), proj_b_ref)
    next(sum_a, None)
    next(sum_b, None)
    next(gram_sum, None)
    next(gram_sum, None)
    next(gram_sum, None)
    next(gram_sum, None)
    for _ in range(4):
        next(sum_a, None)
        next(sum_b, None)


def dma(*shape):
    return pltpu.SemaphoreType.DMA(shape)


def vmem(*shape):
    return pltpu.VMEM(shape, jnp.float32)


def pair(n):
    return dma(2, n)


def sketch_step(embedding, test_matrix):
    rows, width = embedding.shape
    rank = test_matrix.shape[1]
    share = rows // 8
    a, b = 384, rank - 384
    f32 = lambda *shape: jax.ShapeDtypeStruct(shape, jnp.float32)
    scratch = [vmem(rows, width), vmem(width, rank), dma(2)]
    scratch += [vmem(4, 2, share, rank), vmem(4, share, rank), vmem(3, share, rank), pair(4), pair(3)]
    scratch += [vmem(8, share, rank), pair(3), pair(4)]
    scratch += [vmem(width, a), vmem(width, b)]
    scratch += [vmem(width // 4, a), vmem(3, width // 4, a), vmem(7, width // 32, a)]
    scratch += [pair(3), pair(7), pair(7), pair(3)]
    scratch += [vmem(width // 8, b), vmem(7, width // 8, b), vmem(3, width // 32, b)]
    scratch += [pair(7), pair(3), pair(3), pair(7)]
    scratch += [vmem(2, 1024, 128), vmem(256, 128), vmem(32, 128)]
    scratch += [vmem(1024, 128), vmem(3, 256, 128), vmem(7, 32, 128), vmem(4, 32, 128)]
    scratch += [pair(1), pair(3), pair(7), pair(3), pair(7), pair(3), pair(1)]
    return pl.pallas_call(
        sketch_kernel,
        out_shape=(f32(share, rank), f32(width, a), f32(width, b), f32(2, 1024, 128)),
        in_specs=[pl.BlockSpec(memory_space=pl.ANY)] * 2,
        out_specs=[pl.BlockSpec(memory_space=pltpu.VMEM)] * 4,
        scratch_shapes=scratch,
        name="sketch_step",
        compiler_params=pltpu.CompilerParams(
            collective_id=0, has_side_effects=True, vmem_limit_bytes=VMEM_LIMIT
        ),
    )(embedding, test_matrix)


def cols_kernel(part_ref, out_ref, part, by_k, by_x, s_k, s_x, s_gx, s_gk):
    here = place()
    z, y, x, k = here
    barrier, count = enter("kx", here)
    part[...] = part_ref[...]
    pl.semaphore_wait(barrier, count)
    send(part.at[1 - k], by_k, s_k, 0, along("k", here, 1)).wait()
    part[k] = part[k] + by_k[...]
    wait(scatter("x", here, part.at[k], 256, by_x, s_x))
    out_ref[k, pl.ds(x * 256, 256), :] = total(part[k, pl.ds(x * 256, 256), :], by_x)
    wait(gather("x", here, out_ref.at[k], x * 256, 256, s_gx))
    send(out_ref.at[k], out_ref.at[k], s_gk, 0, along("k", here, 1)).wait()


def sum_over_cols(slots):
    return pl.pallas_call(
        cols_kernel,
        out_shape=jax.ShapeDtypeStruct(slots.shape, jnp.float32),
        in_specs=[pl.BlockSpec(memory_space=pltpu.VMEM)],
        out_specs=pl.BlockSpec(memory_space=pltpu.VMEM),
        scratch_shapes=[
            vmem(2, 1024, 128), vmem(1024, 128), vmem(3, 256, 128), pair(1), pair(3), pair(3), pair(1)
        ],
        name="sum_over_cols",
        compiler_params=pltpu.CompilerParams(
            collective_id=1, has_side_effects=True, vmem_limit_bytes=VMEM_LIMIT
        ),
    )(slots)


def load_gram(slots_ref, gram, scale):
    for i in range(5):
        for j in range(i + 1):
            slot = i * (i + 1) // 2 + j
            block = slots_ref[slot // 8, pl.ds((slot % 8) * BLOCK, BLOCK), :]
            gram[pl.ds(i * BLOCK, BLOCK), pl.ds(j * BLOCK, BLOCK)] = block * scale


def factor_and_apply(gram, mats):
    count = gram.shape[0] // BLOCK
    for step in range(count):
        lo, hi = step * BLOCK, (step + 1) * BLOCK
        inverse = invert_factor([gram[lo + TILE * i : lo + TILE * (i + 1), lo:hi] for i in range(TILES)])
        if hi < gram.shape[0]:
            below = dot(gram[hi:, lo:hi], inverse, 1, 1)
            for left in range(hi, gram.shape[0], BLOCK):
                gram[left:, left : left + BLOCK] = gram[left:, left : left + BLOCK] - dot(
                    below[left - hi :], below[left - hi : left - hi + BLOCK], 1, 1
                )
        for mat in mats:
            done = dot(mat[:, lo:hi], inverse, 1, 1)
            mat[:, lo:hi] = done
            if hi < gram.shape[0]:
                mat[:, hi:] = mat[:, hi:] - dot(done, below, 1, 1)


def first_kernel(scale, slots_ref, share_ref, proj_a_ref, proj_b_ref, white_ref, dual_ref, out_ref, gram):
    load_gram(slots_ref, gram, scale)
    white_ref[...] = share_ref[...]
    dual_ref[:, :384] = proj_a_ref[...]
    dual_ref[:, 384:] = proj_b_ref[...]
    factor_and_apply(gram, (white_ref, dual_ref))
    slots_of(dual_ref, out_ref)


def second_kernel(scale, slots_ref, dual_ref, out_ref, gram):
    load_gram(slots_ref, gram, scale)
    out_ref[...] = dual_ref[...]
    factor_and_apply(gram, (out_ref,))


def body(embedding, test_matrix):
    rows_local, width_local = embedding.shape
    total_rows = rows_local * lax.axis_size("rows")
    total_width = width_local * lax.axis_size("cols")
    rank = test_matrix.shape[1]
    f32 = lambda *shape: jax.ShapeDtypeStruct(shape, jnp.float32)
    params = pltpu.CompilerParams(vmem_limit_bytes=VMEM_LIMIT)
    share, proj_a, proj_b, slots = sketch_step(embedding, test_matrix)
    whitened, dual, dual_slots = pl.pallas_call(
        functools.partial(first_kernel, 1.0 / total_rows),
        out_shape=(f32(*share.shape), f32(width_local, rank), f32(2, 1024, 128)),
        scratch_shapes=[vmem(rank, rank)],
        name="whiten_sketch",
        compiler_params=params,
    )(slots, share, proj_a, proj_b)
    col_basis = pl.pallas_call(
        functools.partial(second_kernel, 1.0 / total_width),
        out_shape=f32(width_local, rank),
        scratch_shapes=[vmem(rank, rank)],
        name="whiten_dual",
        compiler_params=params,
    )(sum_over_cols(dual_slots), dual)
    return whitened, col_basis


def solution(mesh):
    placed = (P("rows", "cols"), P("cols", None))
    return jax.shard_map(
        body,
        mesh=mesh,
        in_specs=placed,
        out_specs=(P(("rows", "cols"), None), P("cols", None)),
        check_vma=False,
    )
```

```python
import functools

import jax
import jax.numpy as jnp
from jax import lax
from jax.experimental import pallas as pl
from jax.experimental.pallas import tpu as pltpu
from jax.sharding import PartitionSpec as P

precise = lax.Precision.HIGHEST
BLOCK = 128
TILE = 8
TILES = BLOCK // TILE
NEAR = 4


def dot(left_mat, right_mat, left_dim, right_dim):
    return lax.dot_general(
        left_mat,
        right_mat,
        (((left_dim,), (right_dim,)), ((), ())),
        precision=precise,
        preferred_element_type=jnp.float32,
    )


def invert_factor(rows):
    shape = (TILE, BLOCK)
    lane = lax.broadcasted_iota(jnp.int32, shape, 1)
    sub = lax.broadcasted_iota(jnp.int32, shape, 0)
    rows = list(rows)
    inverse = []
    for tile in range(TILES):
        first = tile * TILE
        near = min(TILES, tile + NEAR)
        here = (lane >= first) & (lane < first + TILE)
        spread = {
            i: [
                jnp.broadcast_to(rows[i][:, col : col + 1], shape)
                for col in range(first, first + TILE)
            ]
            for i in range(tile, near)
        }
        unit = jnp.where(lane - first == sub, 1.0, 0.0)
        for i in range(tile, TILES):
            rows[i] = jnp.where(here, unit if i == tile else 0.0, rows[i])
        pivots = scale = None
        for t in range(TILE):
            pivot = jnp.broadcast_to(spread[tile][t][t : t + 1, :], shape)
            inv_pivot = 1.0 / pivot
            pivots = pivot if t == 0 else jnp.where(sub == t, pivot, pivots)
            scale = inv_pivot if t == 0 else jnp.where(sub == t, inv_pivot, scale)
            pivot_cols = [
                jnp.broadcast_to(spread[tile][u][t : t + 1, :], shape) for u in range(t + 1, TILE)
            ]
            pivot_row = jnp.broadcast_to(rows[tile][t : t + 1, :], shape)
            for i in range(tile, near):
                factor = spread[i][t] * inv_pivot
                if i == tile:
                    factor = jnp.where(sub > t, factor, 0.0)
                for u in range(t + 1, TILE):
                    spread[i][u] = spread[i][u] - factor * pivot_cols[u - t - 1]
                rows[i] = rows[i] - factor * pivot_row
        if near < TILES:
            update = dot(rows[tile] * scale, rows[tile], 0, 0)
            for i in range(near, TILES):
                rows[i] = rows[i] - update[i * TILE : (i + 1) * TILE, :]
        inverse.append(jnp.where(lane < first + TILE, rows[tile], 0.0) * lax.rsqrt(pivots))
    return jnp.concatenate(inverse, 0)


XS, YS, ZS = 4, 4, 8
VMEM_LIMIT = 56 * 2**20


def device(z, y, x, k):
    return {"rows": z * YS + y, "cols": x * 2 + k}


def place():
    r, c = lax.axis_index("rows"), lax.axis_index("cols")
    return r // YS, r % YS, c // 2, c % 2


def along(axis, here, d):
    z, y, x, k = here
    if axis == "z":
        return device((z + d) % ZS, y, x, k)
    if axis == "y":
        return device(z, (y + d) % YS, x, k)
    if axis == "x":
        return device(z, y, (x + d) % XS, k)
    return device(z, y, x, 1 - k)


SIZE = {"z": ZS, "y": YS, "x": XS, "k": 2}


def enter(axes, here):
    barrier = pltpu.get_barrier_semaphore()
    count = 0
    for axis in axes:
        for d in range(1, SIZE[axis]):
            pl.semaphore_signal(
                barrier, inc=1, device_id=along(axis, here, d), device_id_type=pl.DeviceIdType.MESH
            )
            count += 1
    return barrier, count


def send(src, dst, sems, slot, to):
    copy = pltpu.make_async_remote_copy(
        src_ref=src,
        dst_ref=dst,
        send_sem=sems.at[0, slot],
        recv_sem=sems.at[1, slot],
        device_id=to,
        device_id_type=pl.DeviceIdType.MESH,
    )
    copy.start()
    return copy


def scatter(axis, here, src, rows, landing, sems):
    pos = here["zyxk".index(axis)]
    return [
        send(
            src.at[pl.ds(((pos + d) % SIZE[axis]) * rows, rows)],
            landing.at[d - 1],
            sems,
            d - 1,
            along(axis, here, d),
        )
        for d in range(1, SIZE[axis])
    ]


def gather(axis, here, buf, first, rows, sems):
    return [
        send(
            buf.at[pl.ds(first, rows)], buf.at[pl.ds(first, rows)], sems, d - 1, along(axis, here, d)
        )
        for d in range(1, SIZE[axis])
    ]


def wait(copies):
    for copy in copies:
        copy.wait()


def total(first, landing):
    value = first
    for d in range(landing.shape[0]):
        value = value + landing[d]
    return value


def slots_of(mat, out):
    for i in range(5):
        lo = i * BLOCK
        strip = dot(mat[:, lo : lo + BLOCK], mat[:, : lo + BLOCK], 0, 0)
        for j in range(i + 1):
            slot = i * (i + 1) // 2 + j
            out[slot // 8, pl.ds((slot % 8) * BLOCK, BLOCK), :] = strip[:, j * BLOCK : (j + 1) * BLOCK]
    out[1, pl.ds(7 * BLOCK, BLOCK), :] = jnp.zeros((BLOCK, BLOCK), jnp.float32)


def sum_gram(here, part, sums, landings, sems, out):
    z, y, x, k = here
    by_k, by_y, by_z, by_x = landings
    sum_y, sum_z = sums
    rows_y, rows_z = 1024 // YS, 1024 // YS // ZS
    copy = send(part.at[1 - k], by_k, sems["k"], 0, along("k", here, 1))
    yield
    copy.wait()
    part[k] = part[k] + by_k[...]
    copies = scatter("y", here, part.at[k], rows_y, by_y, sems["y"])
    yield
    wait(copies)
    sum_y[...] = total(part[k, pl.ds(y * rows_y, rows_y), :], by_y)
    copies = scatter("z", here, sum_y, rows_z, by_z, sems["z"])
    yield
    wait(copies)
    by_x[x] = total(sum_y[pl.ds(z * rows_z, rows_z), :], by_z)
    copies = [
        send(by_x.at[x], by_x.at[x], sems["x"], d - 1, along("x", here, d)) for d in range(1, XS)
    ]
    yield
    wait(copies)
    first = y * rows_y + z * rows_z
    out[k, pl.ds(first, rows_z), :] = (by_x[0] + by_x[1]) + (by_x[2] + by_x[3])
    copies = gather("z", here, out.at[k], first, rows_z, sems["gz"])
    yield
    wait(copies)
    copies = gather("y", here, out.at[k], y * rows_y, rows_y, sems["gy"])
    yield
    wait(copies)
    copy = send(out.at[k], out.at[k], sems["gk"], 0, along("k", here, 1))
    yield
    copy.wait()


def sum_rows(here, order, part, sum_first, landings, sems, out):
    at = {"z": here[0], "y": here[1]}
    first, second = order
    rows_first = part.shape[0] // SIZE[first]
    rows_second = rows_first // SIZE[second]
    copies = scatter(first, here, part, rows_first, landings[0], sems[0])
    yield
    wait(copies)
    sum_first[...] = total(part[pl.ds(at[first] * rows_first, rows_first), :], landings[0])
    copies = scatter(second, here, sum_first, rows_second, landings[1], sems[1])
    yield
    wait(copies)
    mine = at[first] * rows_first + at[second] * rows_second
    out[pl.ds(mine, rows_second), :] = total(
        sum_first[pl.ds(at[second] * rows_second, rows_second), :], landings[1]
    )
    copies = gather(second, here, out, mine, rows_second, sems[2])
    yield
    wait(copies)
    copies = gather(first, here, out, at[first] * rows_first, rows_first, sems[3])
    yield
    wait(copies)


def sketch_kernel(
    row_scale, emb_hbm, test_hbm,
    share_ref, inverse_ref, dual_ref, slots_ref,
    emb, emb_t, test, load_sems,
    part, by_core, relay, by_x, core_sems, relay_sems, x_sems,
    slab_a, slab_b, gxa_sems, gxb_sems, gka_sems, gkb_sems,
    proj_a, proj_b,
    a_sum, a_in0, a_in1, a_out, a_s0, a_s1, a_s2, a_s3,
    b_sum, b_in0, b_in1, b_out, b_s0, b_s1, b_s2, b_s3,
    gram_part, gram_out, sum_y, sum_z, g_k, g_y, g_z, g_x,
    gs_k, gs_y, gs_z, gs_x, gs_gz, gs_gy, gs_gk,
    gram, dual_part, d_k, d_x, ds_k, ds_x, ds_gx, ds_gk,
):
    here = place()
    z, y, x, k = here
    me = x * 2 + k
    share = part.shape[2]
    half = share // 2
    rows_x = 2 * share
    cut = slab_a.shape[1]
    right, left, sibling = along("x", here, 1), along("x", here, -1), along("k", here, 1)
    barrier, count = enter("kxyz", here)
    load_test = pltpu.make_async_copy(test_hbm, test, load_sems.at[0])
    load_emb = pltpu.make_async_copy(emb_hbm, emb, load_sems.at[1])
    load_test.start()
    load_emb.start()
    load_test.wait()
    load_emb.wait()

    order = (2, 1, 3, 0)
    low, high = pl.ds(0, half), pl.ds(half, half)
    core_copies, relays, arrivals = [], [], []

    def hand_on(step):
        core_copies[step].wait()
        mine = part.at[step, k]
        mine[...] = mine[...] + by_core[step]
        if order[step] == 2:
            relays.append(send(mine.at[low], relay.at[0], relay_sems, 0, right))
            relays.append(send(mine.at[high], relay.at[1], relay_sems, 1, left))
        elif order[step] == 1:
            arrivals.append(send(mine.at[high], by_x.at[0, high], x_sems, 0, right))
            relays[0].wait()
            mine[low, :] = mine[low, :] + relay[0]
            arrivals.append(send(mine.at[low], by_x.at[0, low], x_sems, 1, right))
        elif order[step] == 3:
            arrivals.append(send(mine.at[low], by_x.at[1, low], x_sems, 2, left))
            relays[1].wait()
            mine[high, :] = mine[high, :] + relay[1]
            arrivals.append(send(mine.at[high], by_x.at[1, high], x_sems, 3, left))

    for step, d in enumerate(order):
        target = (x + d) % XS

        @pl.loop(0, 2)
        def _(half):
            first = pl.multiple_of((target * 2 + half) * share, share)
            part[step, half] = dot(emb[pl.ds(first, share), :], test[...], 1, 0)

        if step == 0:
            pl.semaphore_wait(barrier, count)
        core_copies.append(send(part.at[step, 1 - k], by_core.at[step], core_sems, step, sibling))
        if step:
            hand_on(step - 1)
    hand_on(3)

    @pl.loop(0, XS)
    def _(source):
        rows = emb[pl.ds(pl.multiple_of(source * rows_x, rows_x), rows_x), :]
        emb_t[source] = rows.T

    proj_a[...] = jnp.zeros_like(proj_a)
    proj_b[...] = jnp.zeros_like(proj_b)
    wait(arrivals)
    own = part[3, k] + (by_x[0] + by_x[1])
    share_ref[...] = own
    own_rows = pl.ds(pl.multiple_of(me * share, share), share)
    slab_a[own_rows, :] = own[:, :cut]
    slab_b[own_rows, :] = own[:, cut:]

    def piece(slab, source, first, rows):
        return slab.at[pl.ds(pl.multiple_of(source * share, share) + first, rows)]

    def same(slab, sems, slot, source, first, rows, to):
        ref = piece(slab, source, first, rows)
        return send(ref, ref, sems, slot, to)

    def gather_slab(slab, x_sems, core_sems):
        copies = [
            same(slab, x_sems, 0, me, 0, half, right),
            same(slab, x_sems, 1, me, half, half, left),
            same(slab, x_sems, 2, me, half, half, right),
            same(slab, x_sems, 3, me, 0, half, left),
        ]
        across = [same(slab, core_sems, 0, me, 0, share, sibling)]
        before, after, far = [((x + d) % XS) * 2 + k for d in (3, 1, 2)]
        yield across
        copies[0].wait()
        copies.append(same(slab, x_sems, 4, before, 0, half, right))
        copies[1].wait()
        copies.append(same(slab, x_sems, 5, after, half, half, left))
        yield
        copies[2].wait()
        across.append(same(slab, core_sems, 1, before, 0, share, sibling))
        copies[3].wait()
        across.append(same(slab, core_sems, 2, after, 0, share, sibling))
        yield
        copies[4].wait()
        copies[5].wait()
        across.append(same(slab, core_sems, 3, far, 0, share, sibling))
        yield

    def project(across, slab, into, step):
        across[step].wait()
        source = (x + (0, 3, 1, 2)[step]) % XS
        rows = slab[pl.ds(pl.multiple_of(source * rows_x, rows_x), rows_x), :]
        into[...] = into[...] + dot(emb_t[source], rows, 1, 0)

    gather_a = gather_slab(slab_a, gxa_sems, gka_sems)
    across_a = next(gather_a)
    slots_of(share_ref, gram_part)
    gram_sum = sum_gram(
        here, gram_part, (sum_y, sum_z), (g_k, g_y, g_z, g_x),
        dict(k=gs_k, y=gs_y, z=gs_z, x=gs_x, gz=gs_gz, gy=gs_gy, gk=gs_gk), gram_out,
    )
    next(gram_sum, None)
    next(gather_a)
    gather_b = gather_slab(slab_b, gxb_sems, gkb_sems)
    across_b = next(gather_b)
    next(gram_sum, None)
    project(across_a, slab_a, proj_a, 0)
    next(gather_a)
    next(gather_b)
    project(across_a, slab_a, proj_a, 1)
    project(across_a, slab_a, proj_a, 2)
    next(gram_sum, None)
    next(gather_a)
    project(across_b, slab_b, proj_b, 0)
    project(across_a, slab_a, proj_a, 3)
    sum_a = sum_rows(here, "yz", proj_a, a_sum, (a_in0, a_in1), (a_s0, a_s1, a_s2, a_s3), a_out)
    next(sum_a, None)
    next(gather_b)
    next(gram_sum, None)
    project(across_b, slab_b, proj_b, 1)
    project(across_b, slab_b, proj_b, 2)
    next(gather_b)
    next(gram_sum, None)
    project(across_b, slab_b, proj_b, 3)
    sum_b = sum_rows(here, "zy", proj_b, b_sum, (b_in0, b_in1), (b_s0, b_s1, b_s2, b_s3), b_out)
    next(sum_b, None)
    next(gram_sum, None)
    next(sum_a, None)
    next(gram_sum, None)
    next(gram_sum, None)

    load_gram(gram_out, gram, row_scale)
    steps = factor_steps(gram, inverse_ref)
    next(sum_b, None)
    next(steps, None)
    next(sum_a, None)
    next(sum_b, None)
    next(steps, None)
    next(steps, None)
    next(sum_a, None)
    next(sum_b, None)
    next(steps, None)
    next(steps, None)
    next(steps, None)
    next(sum_a, None)
    next(sum_b, None)
    dual_ref[:, :cut] = dot(a_out[...], inverse_ref[:cut, :cut], 1, 1)
    dual_ref[:, cut:] = dot(a_out[...], inverse_ref[cut:, :cut], 1, 1) + dot(
        b_out[...], inverse_ref[cut:, cut:], 1, 1
    )

    slots_of(dual_ref, dual_part)
    send(dual_part.at[1 - k], d_k, ds_k, 0, sibling).wait()
    dual_part[k] = dual_part[k] + d_k[...]
    wait(scatter("x", here, dual_part.at[k], 256, d_x, ds_x))
    slots_ref[k, pl.ds(x * 256, 256), :] = total(dual_part[k, pl.ds(x * 256, 256), :], d_x)
    wait(gather("x", here, slots_ref.at[k], x * 256, 256, ds_gx))
    send(slots_ref.at[k], slots_ref.at[k], ds_gk, 0, sibling).wait()


def dma(*shape):
    return pltpu.SemaphoreType.DMA(shape)


def vmem(*shape):
    return pltpu.VMEM(shape, jnp.float32)


def pair(n):
    return dma(2, n)


def sketch_step(embedding, test_matrix, row_scale):
    rows, width = embedding.shape
    rank = test_matrix.shape[1]
    share = rows // 8
    a, b = 384, rank - 384
    f32 = lambda *shape: jax.ShapeDtypeStruct(shape, jnp.float32)
    scratch = [vmem(rows, width), vmem(XS, width, rows // XS), vmem(width, rank), dma(2)]
    scratch += [vmem(4, 2, share, rank), vmem(4, share, rank), vmem(2, share // 2, rank)]
    scratch += [vmem(2, share, rank), pair(4), pair(2), pair(4)]
    scratch += [vmem(rows, a), vmem(rows, b), pair(6), pair(6), pair(4), pair(4)]
    scratch += [vmem(width, a), vmem(width, b)]
    scratch += [vmem(width // 4, a), vmem(3, width // 4, a), vmem(7, width // 32, a), vmem(width, a)]
    scratch += [pair(3), pair(7), pair(7), pair(3)]
    scratch += [vmem(width // 8, b), vmem(7, width // 8, b), vmem(3, width // 32, b), vmem(width, b)]
    scratch += [pair(7), pair(3), pair(3), pair(7)]
    scratch += [vmem(2, 1024, 128), vmem(2, 1024, 128), vmem(256, 128), vmem(32, 128)]
    scratch += [vmem(1024, 128), vmem(3, 256, 128), vmem(7, 32, 128), vmem(4, 32, 128)]
    scratch += [pair(1), pair(3), pair(7), pair(3), pair(7), pair(3), pair(1)]
    scratch += [vmem(rank, rank), vmem(2, 1024, 128), vmem(1024, 128), vmem(3, 256, 128)]
    scratch += [pair(1), pair(3), pair(3), pair(1)]
    return pl.pallas_call(
        functools.partial(sketch_kernel, row_scale),
        out_shape=(f32(share, rank), f32(rank, rank), f32(width, rank), f32(2, 1024, 128)),
        in_specs=[pl.BlockSpec(memory_space=pl.ANY)] * 2,
        out_specs=[pl.BlockSpec(memory_space=pltpu.VMEM)] * 4,
        scratch_shapes=scratch,
        name="sketch_step",
        compiler_params=pltpu.CompilerParams(
            collective_id=0, has_side_effects=True, vmem_limit_bytes=VMEM_LIMIT
        ),
    )(embedding, test_matrix)


def load_gram(slots_ref, gram, scale):
    for i in range(5):
        for j in range(i + 1):
            slot = i * (i + 1) // 2 + j
            block = slots_ref[slot // 8, pl.ds((slot % 8) * BLOCK, BLOCK), :]
            gram[pl.ds(i * BLOCK, BLOCK), pl.ds(j * BLOCK, BLOCK)] = block * scale


def factor_and_apply(gram, mats):
    count = gram.shape[0] // BLOCK
    for step in range(count):
        lo, hi = step * BLOCK, (step + 1) * BLOCK
        inverse = invert_factor([gram[lo + TILE * i : lo + TILE * (i + 1), lo:hi] for i in range(TILES)])
        if hi < gram.shape[0]:
            below = dot(gram[hi:, lo:hi], inverse, 1, 1)
            for left in range(hi, gram.shape[0], BLOCK):
                gram[left:, left : left + BLOCK] = gram[left:, left : left + BLOCK] - dot(
                    below[left - hi :], below[left - hi : left - hi + BLOCK], 1, 1
                )
        for mat in mats:
            done = dot(mat[:, lo:hi], inverse, 1, 1)
            mat[:, lo:hi] = done
            if hi < gram.shape[0]:
                mat[:, hi:] = mat[:, hi:] - dot(done, below, 1, 1)


def factor_steps(gram, inverse):
    rank = gram.shape[0]
    inverse[...] = jnp.zeros_like(inverse)
    for lo in range(0, rank, BLOCK):
        hi = lo + BLOCK
        if lo:
            ahead = dot(gram[lo:hi, :lo], inverse[:lo, :lo], 1, 0)
        block = invert_factor([gram[lo + TILE * i : lo + TILE * (i + 1), lo:hi] for i in range(TILES)])
        inverse[lo:hi, lo:hi] = block
        if lo:
            inverse[lo:hi, :lo] = -dot(block, ahead, 1, 0)
        if hi < rank:
            below = dot(gram[hi:, lo:hi], block, 1, 1)
            gram[hi:, lo:hi] = below
            for left in range(hi, rank, BLOCK):
                gram[left:, left : left + BLOCK] = gram[left:, left : left + BLOCK] - dot(
                    below[left - hi :], below[left - hi : left - hi + BLOCK], 1, 1
                )
        yield


def last_kernel(scale, slots_ref, dual_ref, share_ref, inverse_ref, white_ref, basis_ref, gram):
    load_gram(slots_ref, gram, scale)
    basis_ref[...] = dual_ref[...]
    white_ref[...] = dot(share_ref[...], inverse_ref[...], 1, 1)
    factor_and_apply(gram, (basis_ref,))


def body(embedding, test_matrix):
    rows_local, width_local = embedding.shape
    total_rows = rows_local * lax.axis_size("rows")
    total_width = width_local * lax.axis_size("cols")
    rank = test_matrix.shape[1]
    f32 = lambda *shape: jax.ShapeDtypeStruct(shape, jnp.float32)
    share, inverse, dual, slots = sketch_step(embedding, test_matrix, 1.0 / total_rows)
    return pl.pallas_call(
        functools.partial(last_kernel, 1.0 / total_width),
        out_shape=(f32(*share.shape), f32(width_local, rank)),
        scratch_shapes=[vmem(rank, rank)],
        name="whiten_both",
        compiler_params=pltpu.CompilerParams(vmem_limit_bytes=VMEM_LIMIT),
    )(slots, dual, share, inverse)


def solution(mesh):
    placed = (P("rows", "cols"), P("cols", None))
    return jax.shard_map(
        body,
        mesh=mesh,
        in_specs=placed,
        out_specs=(P(("rows", "cols"), None), P("cols", None)),
        check_vma=False,
    )
```

```python
import functools

import jax
import jax.numpy as jnp
from jax import lax
from jax.experimental import pallas as pl
from jax.experimental.pallas import tpu as pltpu
from jax.sharding import PartitionSpec as P

precise = lax.Precision.HIGHEST
BLOCK = 128
TILE = 8
TILES = BLOCK // TILE
NEAR = 4


def dot(left_mat, right_mat, left_dim, right_dim):
    return lax.dot_general(
        left_mat,
        right_mat,
        (((left_dim,), (right_dim,)), ((), ())),
        precision=precise,
        preferred_element_type=jnp.float32,
    )


def invert_factor(rows, work=(), hooks={}):
    work = list(work)
    shape = (TILE, BLOCK)
    lane = lax.broadcasted_iota(jnp.int32, shape, 1)
    sub = lax.broadcasted_iota(jnp.int32, shape, 0)
    rows = list(rows)
    inverse = []
    for tile in range(TILES):
        first = tile * TILE
        near = min(TILES, tile + NEAR)
        here = (lane >= first) & (lane < first + TILE)
        spread = {
            i: [
                jnp.broadcast_to(rows[i][:, col : col + 1], shape)
                for col in range(first, first + TILE)
            ]
            for i in range(tile, near)
        }
        unit = jnp.where(lane - first == sub, 1.0, 0.0)
        for i in range(tile, TILES):
            rows[i] = jnp.where(here, unit if i == tile else 0.0, rows[i])
        pivots = scale = None
        for t in range(TILE):
            pivot = jnp.broadcast_to(spread[tile][t][t : t + 1, :], shape)
            inv_pivot = 1.0 / pivot
            pivots = pivot if t == 0 else jnp.where(sub == t, pivot, pivots)
            scale = inv_pivot if t == 0 else jnp.where(sub == t, inv_pivot, scale)
            pivot_cols = [
                jnp.broadcast_to(spread[tile][u][t : t + 1, :], shape) for u in range(t + 1, TILE)
            ]
            pivot_row = jnp.broadcast_to(rows[tile][t : t + 1, :], shape)
            for i in range(tile, near):
                factor = spread[i][t] * inv_pivot
                if i == tile:
                    factor = jnp.where(sub > t, factor, 0.0)
                for u in range(t + 1, TILE):
                    spread[i][u] = spread[i][u] - factor * pivot_cols[u - t - 1]
                rows[i] = rows[i] - factor * pivot_row
        if near < TILES:
            update = dot(rows[tile] * scale, rows[tile], 0, 0)
            for i in range(near, TILES):
                rows[i] = rows[i] - update[i * TILE : (i + 1) * TILE, :]
        inverse.append(jnp.where(lane < first + TILE, rows[tile], 0.0) * lax.rsqrt(pivots))
        for _ in range(-(-len(work) // (TILES - tile))):
            work.pop(0)()
        if tile in hooks:
            hooks[tile]()
    return jnp.concatenate(inverse, 0)


XS, YS, ZS = 4, 4, 8
VMEM_LIMIT = 56 * 2**20


def device(z, y, x, k):
    return {"rows": z * YS + y, "cols": x * 2 + k}


def place():
    r, c = lax.axis_index("rows"), lax.axis_index("cols")
    return r // YS, r % YS, c // 2, c % 2


def along(axis, here, d):
    z, y, x, k = here
    if axis == "z":
        return device((z + d) % ZS, y, x, k)
    if axis == "y":
        return device(z, (y + d) % YS, x, k)
    if axis == "x":
        return device(z, y, (x + d) % XS, k)
    return device(z, y, x, 1 - k)


SIZE = {"z": ZS, "y": YS, "x": XS, "k": 2}


def plane(here):
    z, y, x, k = here
    return [
        device(z, (y + i) % YS, (x + j) % XS, k) for i in range(YS) for j in range(XS) if i or j
    ]


def enter(axes, here):
    barrier = pltpu.get_barrier_semaphore()
    peers = plane(here)
    for peer in peers:
        pl.semaphore_signal(barrier, inc=1, device_id=peer, device_id_type=pl.DeviceIdType.MESH)
    count = len(peers)
    for axis in axes:
        for d in range(1, SIZE[axis]):
            pl.semaphore_signal(
                barrier, inc=1, device_id=along(axis, here, d), device_id_type=pl.DeviceIdType.MESH
            )
            count += 1
    return barrier, count


def send(src, dst, sems, slot, to):
    copy = pltpu.make_async_remote_copy(
        src_ref=src,
        dst_ref=dst,
        send_sem=sems.at[0, slot],
        recv_sem=sems.at[1, slot],
        device_id=to,
        device_id_type=pl.DeviceIdType.MESH,
    )
    copy.start()
    return copy


def scatter(axis, here, src, rows, landing, sems):
    pos = here["zyxk".index(axis)]
    return [
        send(
            src.at[pl.ds(((pos + d) % SIZE[axis]) * rows, rows)],
            landing.at[d - 1],
            sems,
            d - 1,
            along(axis, here, d),
        )
        for d in range(1, SIZE[axis])
    ]


def gather(axis, here, buf, first, rows, sems):
    return [
        send(
            buf.at[pl.ds(first, rows)], buf.at[pl.ds(first, rows)], sems, d - 1, along(axis, here, d)
        )
        for d in range(1, SIZE[axis])
    ]


def wait(copies):
    for copy in copies:
        copy.wait()


def total(first, landing):
    value = first
    for d in range(landing.shape[0]):
        value = value + landing[d]
    return value


def slots_of(mat, out):
    for i in range(5):
        lo = i * BLOCK
        strip = dot(mat[:, lo : lo + BLOCK], mat[:, : lo + BLOCK], 0, 0)
        for j in range(i + 1):
            slot = i * (i + 1) // 2 + j
            out[slot // 8, pl.ds((slot % 8) * BLOCK, BLOCK), :] = strip[:, j * BLOCK : (j + 1) * BLOCK]
    out[1, pl.ds(7 * BLOCK, BLOCK), :] = jnp.zeros((BLOCK, BLOCK), jnp.float32)


def sum_gram(here, part, sums, landings, sems, out):
    z, y, x, k = here
    by_k, by_y, by_z, by_x = landings
    sum_y, sum_z = sums
    rows_y, rows_z = 1024 // YS, 1024 // YS // ZS
    copy = send(part.at[1 - k], by_k, sems["k"], 0, along("k", here, 1))
    yield
    copy.wait()
    part[k] = part[k] + by_k[...]
    copies = scatter("y", here, part.at[k], rows_y, by_y, sems["y"])
    yield
    wait(copies)
    sum_y[...] = total(part[k, pl.ds(y * rows_y, rows_y), :], by_y)
    copies = scatter("z", here, sum_y, rows_z, by_z, sems["z"])
    yield
    wait(copies)
    by_x[x] = total(sum_y[pl.ds(z * rows_z, rows_z), :], by_z)
    copies = [
        send(by_x.at[x], by_x.at[x], sems["x"], d - 1, along("x", here, d)) for d in range(1, XS)
    ]
    yield
    wait(copies)
    first = y * rows_y + z * rows_z
    out[k, pl.ds(first, rows_z), :] = (by_x[0] + by_x[1]) + (by_x[2] + by_x[3])
    copies = gather("z", here, out.at[k], first, rows_z, sems["gz"])
    yield
    wait(copies)
    copies = gather("y", here, out.at[k], y * rows_y, rows_y, sems["gy"])
    yield
    wait(copies)
    copy = send(out.at[k], out.at[k], sems["gk"], 0, along("k", here, 1))
    yield
    copy.wait()


def sum_rows(here, order, part, sum_first, landings, sems, out):
    at = {"z": here[0], "y": here[1]}
    first, second = order
    rows_first = part.shape[0] // SIZE[first]
    rows_second = rows_first // SIZE[second]
    copies = scatter(first, here, part, rows_first, landings[0], sems[0])
    yield
    wait(copies)
    sum_first[...] = total(part[pl.ds(at[first] * rows_first, rows_first), :], landings[0])
    copies = scatter(second, here, sum_first, rows_second, landings[1], sems[1])
    yield
    wait(copies)
    mine = at[first] * rows_first + at[second] * rows_second
    out[pl.ds(mine, rows_second), :] = total(
        sum_first[pl.ds(at[second] * rows_second, rows_second), :], landings[1]
    )
    copies = gather(second, here, out, mine, rows_second, sems[2])
    yield
    wait(copies)
    copies = gather(first, here, out, at[first] * rows_first, rows_first, sems[3])
    yield
    wait(copies)


def sketch_kernel(
    row_scale, emb_hbm, test_hbm,
    share_ref, inverse_ref, dual_ref, slots_ref,
    emb, emb_t, test, load_sems,
    part, by_core, relay, by_x, core_sems, relay_sems, x_sems,
    slab_a, slab_b, gxa_sems, gxb_sems, gka_sems, gkb_sems,
    proj_a, proj_b,
    a_sum, a_in0, a_in1, a_out, a_s0, a_s1, a_s2, a_s3,
    b_sum, b_in0, b_in1, b_out, b_s0, b_s1, b_s2, b_s3,
    c_sum, c_in0, c_in1, c_out, c_s0, c_s1, c_s2, c_s3,
    gram_part, gram_out, sum_y, sum_z, g_k, g_y, g_z, g_x,
    gs_k, gs_y, gs_z, gs_x, gs_gz, gs_gy, gs_gk,
    gram, dual_cols, dual_part, d_k, d_sum, d_x, ds_k, ds_x, ds_gxy, ds_gk,
):
    here = place()
    z, y, x, k = here
    me = x * 2 + k
    share = part.shape[2]
    half = share // 2
    rows_x = 2 * share
    cut = slab_a.shape[1]
    right, left, sibling = along("x", here, 1), along("x", here, -1), along("k", here, 1)
    barrier, count = enter("kz", here)
    load_test = pltpu.make_async_copy(test_hbm, test, load_sems.at[0])
    load_emb = pltpu.make_async_copy(emb_hbm, emb, load_sems.at[1])
    load_test.start()
    load_emb.start()
    load_test.wait()
    load_emb.wait()

    order = (2, 1, 3, 0)
    low, high = pl.ds(0, half), pl.ds(half, half)
    core_copies, relays, arrivals = [], [], []

    def hand_on(step):
        core_copies[step].wait()
        mine = part.at[step, k]
        mine[...] = mine[...] + by_core[step]
        if order[step] == 2:
            relays.append(send(mine.at[low], relay.at[0], relay_sems, 0, right))
            relays.append(send(mine.at[high], relay.at[1], relay_sems, 1, left))
        elif order[step] == 1:
            arrivals.append(send(mine.at[high], by_x.at[0, high], x_sems, 0, right))
            relays[0].wait()
            mine[low, :] = mine[low, :] + relay[0]
            arrivals.append(send(mine.at[low], by_x.at[0, low], x_sems, 1, right))
        elif order[step] == 3:
            arrivals.append(send(mine.at[low], by_x.at[1, low], x_sems, 2, left))
            relays[1].wait()
            mine[high, :] = mine[high, :] + relay[1]
            arrivals.append(send(mine.at[high], by_x.at[1, high], x_sems, 3, left))

    for step, d in enumerate(order):
        target = (x + d) % XS

        @pl.loop(0, 2)
        def _(half):
            first = pl.multiple_of((target * 2 + half) * share, share)
            part[step, half] = dot(emb[pl.ds(first, share), :], test[...], 1, 0)

        if step == 0:
            pl.semaphore_wait(barrier, count)
        core_copies.append(send(part.at[step, 1 - k], by_core.at[step], core_sems, step, sibling))
        if step:
            hand_on(step - 1)
    hand_on(3)

    @pl.loop(0, XS)
    def _(source):
        rows = emb[pl.ds(pl.multiple_of(source * rows_x, rows_x), rows_x), :]
        emb_t[source] = rows.T

    proj_a[...] = jnp.zeros_like(proj_a)
    proj_b[...] = jnp.zeros_like(proj_b)
    wait(arrivals)
    own = part[3, k] + (by_x[0] + by_x[1])
    share_ref[...] = own
    own_rows = pl.ds(pl.multiple_of(me * share, share), share)
    slab_a[own_rows, :] = own[:, :cut]
    slab_b[own_rows, :] = own[:, cut:]

    def piece(slab, source, first, rows):
        return slab.at[pl.ds(pl.multiple_of(source * share, share) + first, rows)]

    def same(slab, sems, slot, source, first, rows, to):
        ref = piece(slab, source, first, rows)
        return send(ref, ref, sems, slot, to)

    def gather_slab(slab, x_sems, core_sems):
        copies = [
            same(slab, x_sems, 0, me, 0, half, right),
            same(slab, x_sems, 1, me, half, half, left),
            same(slab, x_sems, 2, me, half, half, right),
            same(slab, x_sems, 3, me, 0, half, left),
        ]
        across = [same(slab, core_sems, 0, me, 0, share, sibling)]
        before, after, far = [((x + d) % XS) * 2 + k for d in (3, 1, 2)]
        yield across
        copies[0].wait()
        copies.append(same(slab, x_sems, 4, before, 0, half, right))
        copies[1].wait()
        copies.append(same(slab, x_sems, 5, after, half, half, left))
        yield
        copies[2].wait()
        across.append(same(slab, core_sems, 1, before, 0, share, sibling))
        copies[3].wait()
        across.append(same(slab, core_sems, 2, after, 0, share, sibling))
        yield
        copies[4].wait()
        copies[5].wait()
        across.append(same(slab, core_sems, 3, far, 0, share, sibling))
        yield

    def project(across, slab, into, step):
        across[step].wait()
        source = (x + (0, 3, 1, 2)[step]) % XS
        rows = slab[pl.ds(pl.multiple_of(source * rows_x, rows_x), rows_x), :]
        into[...] = into[...] + dot(emb_t[source], rows, 1, 0)

    gather_a = gather_slab(slab_a, gxa_sems, gka_sems)
    across_a = next(gather_a)
    slots_of(share_ref, gram_part)
    gram_sum = sum_gram(
        here, gram_part, (sum_y, sum_z), (g_k, g_y, g_z, g_x),
        dict(k=gs_k, y=gs_y, z=gs_z, x=gs_x, gz=gs_gz, gy=gs_gy, gk=gs_gk), gram_out,
    )
    next(gram_sum, None)
    next(gram_sum, None)
    next(gather_a)
    gather_b = gather_slab(slab_b, gxb_sems, gkb_sems)
    across_b = next(gather_b)
    project(across_a, slab_a, proj_a, 0)
    next(gather_a)
    next(gather_a)
    project(across_a, slab_a, proj_a, 1)
    next(gram_sum, None)
    next(gather_b)
    project(across_a, slab_a, proj_a, 2)
    project(across_a, slab_a, proj_a, 3)
    sum_a = sum_rows(here, "yz", proj_a, a_sum, (a_in0, a_in1), (a_s0, a_s1, a_s2, a_s3), a_out)
    next(sum_a, None)
    project(across_b, slab_b, proj_b, 0)
    next(gather_b)
    next(gram_sum, None)
    next(gather_b)
    project(across_b, slab_b, proj_b, 1)
    project(across_b, slab_b, proj_b, 2)
    next(gram_sum, None)
    project(across_b, slab_b, proj_b, 3)
    middle = slab_b.shape[1] // 2
    sum_c = sum_rows(
        here, "yz", proj_b.at[:, :middle], c_sum, (c_in0, c_in1), (c_s0, c_s1, c_s2, c_s3), c_out
    )
    sum_b = sum_rows(
        here, "zy", proj_b.at[:, middle:], b_sum, (b_in0, b_in1), (b_s0, b_s1, b_s2, b_s3), b_out
    )
    next(sum_b, None)
    next(sum_c, None)
    next(gram_sum, None)
    next(sum_a, None)
    next(sum_c, None)
    next(gram_sum, None)
    next(sum_b, None)
    next(gram_sum, None)

    load_gram(gram_out, gram, row_scale)
    step_a, step_b, step_c = [functools.partial(next, item, None) for item in (sum_a, sum_b, sum_c)]
    hooks = {
        0: {4: step_a, 9: step_b, 10: step_c},
        1: {6: step_b, 15: step_a},
        2: {6: step_c},
    }
    for _ in factor_steps(gram, inverse_ref, hooks=hooks):
        pass
    step_a()
    step_b()
    step_c()
    far = cut + middle
    dual_ref[:, :cut] = dot(a_out[...], inverse_ref[:cut, :cut], 1, 1)
    dual_ref[:, cut:] = (
        dot(a_out[...], inverse_ref[cut:, :cut], 1, 1)
        + dot(c_out[...], inverse_ref[cut:, cut:far], 1, 1)
        + dot(b_out[...], inverse_ref[cut:, far:], 1, 1)
    )

    for i in range(dual_cols.shape[0]):
        dual_cols[i] = dual_ref[:, i * BLOCK : (i + 1) * BLOCK]
    for i in range(4):
        row, col = block_of(4 * y + i)
        dual_part[pl.ds(i * BLOCK, BLOCK), :] = dot(
            dual_cols[jnp.maximum(row, col)], dual_cols[jnp.minimum(row, col)], 0, 0
        )
    mine = pl.ds(pl.multiple_of(k * 256, 256), 256)
    theirs = pl.ds(pl.multiple_of((1 - k) * 256, 256), 256)
    send(dual_part.at[theirs], d_k, ds_k, 0, sibling).wait()
    d_sum[...] = dual_part[mine, :] + d_k[...]
    wait(scatter("x", here, d_sum, 64, d_x, ds_x))
    done = pl.ds(pl.multiple_of(y * 512 + k * 256 + x * 64, 64), 64)
    slots_ref[done, :] = total(d_sum[pl.ds(pl.multiple_of(x * 64, 64), 64), :], d_x)
    wait(
        [
            send(slots_ref.at[done], slots_ref.at[done], ds_gxy, i, peer)
            for i, peer in enumerate(plane(here))
        ]
    )
    copies = []
    for i in range(YS):
        both = pl.ds(pl.multiple_of(i * 512 + k * 256, 256), 256)
        copies.append(send(slots_ref.at[both], slots_ref.at[both], ds_gk, i, sibling))
    wait(copies)


def block_of(slot):
    return slot % 5, (slot % 5 + slot // 5) % 5


def dma(*shape):
    return pltpu.SemaphoreType.DMA(shape)


def vmem(*shape):
    return pltpu.VMEM(shape, jnp.float32)


def pair(n):
    return dma(2, n)


def sketch_step(embedding, test_matrix, row_scale):
    rows, width = embedding.shape
    rank = test_matrix.shape[1]
    share = rows // 8
    a, b = 384, rank - 384
    f32 = lambda *shape: jax.ShapeDtypeStruct(shape, jnp.float32)
    scratch = [vmem(rows, width), vmem(XS, width, rows // XS), vmem(width, rank), dma(2)]
    scratch += [vmem(4, 2, share, rank), vmem(4, share, rank), vmem(2, share // 2, rank)]
    scratch += [vmem(2, share, rank), pair(4), pair(2), pair(4)]
    scratch += [vmem(rows, a), vmem(rows, b), pair(6), pair(6), pair(4), pair(4)]
    scratch += [vmem(width, a), vmem(width, b)]
    scratch += [vmem(width // 4, a), vmem(3, width // 4, a), vmem(7, width // 32, a), vmem(width, a)]
    scratch += [pair(3), pair(7), pair(7), pair(3)]
    c = b // 2
    scratch += [vmem(width // 8, c), vmem(7, width // 8, c), vmem(3, width // 32, c), vmem(width, c)]
    scratch += [pair(7), pair(3), pair(3), pair(7)]
    scratch += [vmem(width // 4, c), vmem(3, width // 4, c), vmem(7, width // 32, c), vmem(width, c)]
    scratch += [pair(3), pair(7), pair(7), pair(3)]
    scratch += [vmem(2, 1024, 128), vmem(2, 1024, 128), vmem(256, 128), vmem(32, 128)]
    scratch += [vmem(1024, 128), vmem(3, 256, 128), vmem(7, 32, 128), vmem(4, 32, 128)]
    scratch += [pair(1), pair(3), pair(7), pair(3), pair(7), pair(3), pair(1)]
    scratch += [vmem(rank, rank), vmem(rank // BLOCK, width, BLOCK), vmem(512, 128)]
    scratch += [vmem(256, 128), vmem(256, 128), vmem(3, 64, 128)]
    scratch += [pair(1), pair(3), pair(YS * XS - 1), pair(YS)]
    return pl.pallas_call(
        functools.partial(sketch_kernel, row_scale),
        out_shape=(f32(share, rank), f32(rank, rank), f32(width, rank), f32(2048, 128)),
        in_specs=[pl.BlockSpec(memory_space=pl.ANY)] * 2,
        out_specs=[pl.BlockSpec(memory_space=pltpu.VMEM)] * 4,
        scratch_shapes=scratch,
        name="sketch_step",
        compiler_params=pltpu.CompilerParams(
            collective_id=0, has_side_effects=True, vmem_limit_bytes=VMEM_LIMIT
        ),
    )(embedding, test_matrix)


def load_gram(slots_ref, gram, scale):
    for i in range(5):
        for j in range(i + 1):
            slot = i * (i + 1) // 2 + j
            block = slots_ref[slot // 8, pl.ds((slot % 8) * BLOCK, BLOCK), :]
            gram[pl.ds(i * BLOCK, BLOCK), pl.ds(j * BLOCK, BLOCK)] = block * scale


def factor_steps(gram, inverse=None, mats=(), work=(), hooks={}):
    rank = gram.shape[0]
    work = list(work)
    ahead = {}
    if inverse is not None:
        inverse[...] = jnp.zeros_like(inverse)

    def update(rows, cols, lo):
        source = slice(lo, lo + BLOCK)
        gram[rows, cols] = gram[rows, cols] - dot(gram[rows, source], gram[cols, source], 1, 1)

    def solve(rows, lo, block):
        gram[rows, lo : lo + BLOCK] = dot(gram[rows, lo : lo + BLOCK], block, 1, 1)

    def apply(mat, lo, block):
        mat[:, lo : lo + BLOCK] = dot(mat[:, lo : lo + BLOCK], block, 1, 1)

    def reduce(mat, cols, lo):
        source = slice(lo, lo + BLOCK)
        mat[:, cols] = mat[:, cols] - dot(mat[:, source], gram[cols, source], 1, 1)

    def finish(lo, block):
        inverse[lo : lo + BLOCK, :lo] = -dot(block, ahead[lo], 1, 0)

    def prepare(lo):
        ahead[lo] = dot(gram[lo : lo + BLOCK, :lo], inverse[:lo, :lo], 1, 0)

    call = functools.partial
    for lo in range(0, rank, BLOCK):
        hi = lo + BLOCK
        tiles = [gram[lo + TILE * i : lo + TILE * (i + 1), lo:hi] for i in range(TILES)]
        block = invert_factor(tiles, work, hooks.get(lo // BLOCK, {}))
        work = []
        following = [slice(i, i + BLOCK) for i in range(hi, rank, BLOCK)]
        if following:
            solve(following[0], lo, block)
            update(following[0], following[0], lo)
        if following[1:]:
            work.append(call(solve, slice(hi + BLOCK, rank), lo, block))
            work.append(call(update, slice(hi + BLOCK, rank), following[0], lo))
            work += [call(update, slice(cols.start, rank), cols, lo) for cols in following[1:]]
        if inverse is not None:
            inverse[lo:hi, lo:hi] = block
            if lo:
                work.append(call(finish, lo, block))
            if following:
                work.append(call(prepare, hi))
        for mat in mats:
            work.append(call(apply, mat, lo, block))
            work += [call(reduce, mat, cols, lo) for cols in following]
        if not following:
            for item in work:
                item()
        yield


def last_kernel(scale, slots_ref, dual_ref, share_ref, inverse_ref, white_ref, basis_ref, gram):
    for slot in range(15):
        row, col = block_of(slot)
        row, col = max(row, col), min(row, col)
        gram[row * BLOCK : (row + 1) * BLOCK, col * BLOCK : (col + 1) * BLOCK] = (
            slots_ref[slot * BLOCK : (slot + 1) * BLOCK, :] * scale
        )
    basis_ref[...] = dual_ref[...]

    def whiten(cols):
        white_ref[:, cols] = dot(share_ref[...], inverse_ref[cols, :], 1, 1)

    work = [functools.partial(whiten, slice(i, i + BLOCK)) for i in range(0, gram.shape[0], BLOCK)]
    for _ in factor_steps(gram, mats=(basis_ref,), work=work):
        pass


def body(embedding, test_matrix):
    rows_local, width_local = embedding.shape
    total_rows = rows_local * lax.axis_size("rows")
    total_width = width_local * lax.axis_size("cols")
    rank = test_matrix.shape[1]
    f32 = lambda *shape: jax.ShapeDtypeStruct(shape, jnp.float32)
    share, inverse, dual, slots = sketch_step(embedding, test_matrix, 1.0 / total_rows)
    return pl.pallas_call(
        functools.partial(last_kernel, 1.0 / total_width),
        out_shape=(f32(*share.shape), f32(width_local, rank)),
        scratch_shapes=[vmem(rank, rank)],
        name="whiten_both",
        compiler_params=pltpu.CompilerParams(vmem_limit_bytes=VMEM_LIMIT),
    )(slots, dual, share, inverse)


def solution(mesh):
    placed = (P("rows", "cols"), P("cols", None))
    return jax.shard_map(
        body,
        mesh=mesh,
        in_specs=placed,
        out_specs=(P(("rows", "cols"), None), P("cols", None)),
        check_vma=False,
    )
```

```python
import functools

import jax
import jax.numpy as jnp
from jax import lax
from jax.experimental import pallas as pl
from jax.experimental.pallas import tpu as pltpu
from jax.sharding import PartitionSpec as P

precise = lax.Precision.HIGHEST
BLOCK = 128
TILE = 8
TILES = BLOCK // TILE
NEAR = 4


def dot(left_mat, right_mat, left_dim, right_dim):
    return lax.dot_general(
        left_mat,
        right_mat,
        (((left_dim,), (right_dim,)), ((), ())),
        precision=precise,
        preferred_element_type=jnp.float32,
    )


def invert_factor(rows, work=(), hooks={}):
    work = list(work)
    shape = (TILE, BLOCK)
    lane = lax.broadcasted_iota(jnp.int32, shape, 1)
    sub = lax.broadcasted_iota(jnp.int32, shape, 0)
    rows = list(rows)
    inverse = []
    for tile in range(TILES):
        first = tile * TILE
        near = min(TILES, tile + NEAR)
        here = (lane >= first) & (lane < first + TILE)
        spread = {
            i: [
                jnp.broadcast_to(rows[i][:, col : col + 1], shape)
                for col in range(first, first + TILE)
            ]
            for i in range(tile, near)
        }
        unit = jnp.where(lane - first == sub, 1.0, 0.0)
        for i in range(tile, TILES):
            rows[i] = jnp.where(here, unit if i == tile else 0.0, rows[i])
        pivots = scale = None
        for t in range(TILE):
            pivot = jnp.broadcast_to(spread[tile][t][t : t + 1, :], shape)
            inv_pivot = 1.0 / pivot
            pivots = pivot if t == 0 else jnp.where(sub == t, pivot, pivots)
            scale = inv_pivot if t == 0 else jnp.where(sub == t, inv_pivot, scale)
            pivot_cols = [
                jnp.broadcast_to(spread[tile][u][t : t + 1, :], shape) for u in range(t + 1, TILE)
            ]
            pivot_row = jnp.broadcast_to(rows[tile][t : t + 1, :], shape)
            for i in range(tile, near):
                factor = spread[i][t] * inv_pivot
                if i == tile:
                    factor = jnp.where(sub > t, factor, 0.0)
                for u in range(t + 1, TILE):
                    spread[i][u] = spread[i][u] - factor * pivot_cols[u - t - 1]
                rows[i] = rows[i] - factor * pivot_row
        if near < TILES:
            update = dot(rows[tile] * scale, rows[tile], 0, 0)
            for i in range(near, TILES):
                rows[i] = rows[i] - update[i * TILE : (i + 1) * TILE, :]
        inverse.append(jnp.where(lane < first + TILE, rows[tile], 0.0) * lax.rsqrt(pivots))
        for _ in range(-(-len(work) // (TILES - tile))):
            work.pop(0)()
        if tile in hooks:
            hooks[tile]()
    return jnp.concatenate(inverse, 0)


XS, YS, ZS = 4, 4, 8
VMEM_LIMIT = 56 * 2**20


def device(z, y, x, k):
    return {"rows": z * YS + y, "cols": x * 2 + k}


def place():
    r, c = lax.axis_index("rows"), lax.axis_index("cols")
    return r // YS, r % YS, c // 2, c % 2


def along(axis, here, d):
    z, y, x, k = here
    if axis == "z":
        return device((z + d) % ZS, y, x, k)
    if axis == "y":
        return device(z, (y + d) % YS, x, k)
    if axis == "x":
        return device(z, y, (x + d) % XS, k)
    return device(z, y, x, 1 - k)


SIZE = {"z": ZS, "y": YS, "x": XS, "k": 2}


def plane(here):
    z, y, x, k = here
    return [
        device(z, (y + i) % YS, (x + j) % XS, k) for i in range(YS) for j in range(XS) if i or j
    ]


def enter(axes, here):
    barrier = pltpu.get_barrier_semaphore()
    peers = plane(here)
    for peer in peers:
        pl.semaphore_signal(barrier, inc=1, device_id=peer, device_id_type=pl.DeviceIdType.MESH)
    count = len(peers)
    for axis in axes:
        for d in range(1, SIZE[axis]):
            pl.semaphore_signal(
                barrier, inc=1, device_id=along(axis, here, d), device_id_type=pl.DeviceIdType.MESH
            )
            count += 1
    return barrier, count


def send(src, dst, sems, slot, to):
    copy = pltpu.make_async_remote_copy(
        src_ref=src,
        dst_ref=dst,
        send_sem=sems.at[0, slot],
        recv_sem=sems.at[1, slot],
        device_id=to,
        device_id_type=pl.DeviceIdType.MESH,
    )
    copy.start()
    return copy


def scatter(axis, here, src, rows, landing, sems):
    pos = here["zyxk".index(axis)]
    return [
        send(
            src.at[pl.ds(((pos + d) % SIZE[axis]) * rows, rows)],
            landing.at[d - 1],
            sems,
            d - 1,
            along(axis, here, d),
        )
        for d in range(1, SIZE[axis])
    ]


def gather(axis, here, buf, first, rows, sems):
    return [
        send(
            buf.at[pl.ds(first, rows)], buf.at[pl.ds(first, rows)], sems, d - 1, along(axis, here, d)
        )
        for d in range(1, SIZE[axis])
    ]


def wait(copies):
    for copy in copies:
        copy.wait()


def total(first, landing):
    value = first
    for d in range(landing.shape[0]):
        value = value + landing[d]
    return value


def slots_of(mat, out):
    for i in range(5):
        lo = i * BLOCK
        strip = dot(mat[:, lo : lo + BLOCK], mat[:, : lo + BLOCK], 0, 0)
        for j in range(i + 1):
            slot = i * (i + 1) // 2 + j
            out[slot // 8, pl.ds((slot % 8) * BLOCK, BLOCK), :] = strip[:, j * BLOCK : (j + 1) * BLOCK]
    out[1, pl.ds(7 * BLOCK, BLOCK), :] = jnp.zeros((BLOCK, BLOCK), jnp.float32)


def sum_gram(here, part, sums, landings, sems, out):
    z, y, x, k = here
    by_k, by_y, by_z, by_x = landings
    sum_y, sum_z = sums
    rows_y, rows_z = 1024 // YS, 1024 // YS // ZS
    copy = send(part.at[1 - k], by_k, sems["k"], 0, along("k", here, 1))
    yield
    copy.wait()
    part[k] = part[k] + by_k[...]
    copies = scatter("y", here, part.at[k], rows_y, by_y, sems["y"])
    yield
    wait(copies)
    sum_y[...] = total(part[k, pl.ds(y * rows_y, rows_y), :], by_y)
    copies = scatter("z", here, sum_y, rows_z, by_z, sems["z"])
    yield
    wait(copies)
    by_x[x] = total(sum_y[pl.ds(z * rows_z, rows_z), :], by_z)
    copies = [
        send(by_x.at[x], by_x.at[x], sems["x"], d - 1, along("x", here, d)) for d in range(1, XS)
    ]
    yield
    wait(copies)
    first = y * rows_y + z * rows_z
    out[k, pl.ds(first, rows_z), :] = (by_x[0] + by_x[1]) + (by_x[2] + by_x[3])
    copies = gather("z", here, out.at[k], first, rows_z, sems["gz"])
    yield
    wait(copies)
    copies = gather("y", here, out.at[k], y * rows_y, rows_y, sems["gy"])
    yield
    wait(copies)
    copy = send(out.at[k], out.at[k], sems["gk"], 0, along("k", here, 1))
    yield
    copy.wait()


def sum_rows(here, order, part, sum_first, landings, sems, out):
    at = {"z": here[0], "y": here[1]}
    first, second = order
    rows_first = part.shape[0] // SIZE[first]
    rows_second = rows_first // SIZE[second]
    copies = scatter(first, here, part, rows_first, landings[0], sems[0])
    yield
    wait(copies)
    sum_first[...] = total(part[pl.ds(at[first] * rows_first, rows_first), :], landings[0])
    copies = scatter(second, here, sum_first, rows_second, landings[1], sems[1])
    yield
    wait(copies)
    mine = at[first] * rows_first + at[second] * rows_second
    out[pl.ds(mine, rows_second), :] = total(
        sum_first[pl.ds(at[second] * rows_second, rows_second), :], landings[1]
    )
    copies = gather(second, here, out, mine, rows_second, sems[2])
    yield
    wait(copies)
    copies = gather(first, here, out, at[first] * rows_first, rows_first, sems[3])
    yield
    wait(copies)


def sketch_kernel(
    row_scale, emb_hbm, test_hbm,
    share_out, inverse_out, dual_out, slots_ref,
    share_ref, inverse_ref, dual_ref, store_sems,
    emb, emb_t, test, load_sems,
    part, by_core, relay, by_x, core_sems, relay_sems, x_sems,
    slab_a, slab_b, gxa_sems, gxb_sems, gka_sems, gkb_sems,
    proj_a, proj_b,
    a_sum, a_in0, a_in1, a_out, a_s0, a_s1, a_s2, a_s3,
    b_sum, b_in0, b_in1, b_out, b_s0, b_s1, b_s2, b_s3,
    c_sum, c_in0, c_in1, c_out, c_s0, c_s1, c_s2, c_s3,
    gram_part, gram_out, sum_y, sum_z, g_k, g_y, g_z, g_x,
    gs_k, gs_y, gs_z, gs_x, gs_gz, gs_gy, gs_gk,
    gram, dual_cols, dual_part, d_k, d_sum, d_x, ds_k, ds_x, ds_gxy, ds_gk,
):
    here = place()
    z, y, x, k = here
    me = x * 2 + k
    share = part.shape[2]
    half = share // 2
    rows_x = 2 * share
    cut = slab_a.shape[1]
    right, left, sibling = along("x", here, 1), along("x", here, -1), along("k", here, 1)
    barrier, count = enter("kz", here)
    load_test = pltpu.make_async_copy(test_hbm, test, load_sems.at[0])
    load_emb = pltpu.make_async_copy(emb_hbm, emb, load_sems.at[1])
    load_test.start()
    load_emb.start()
    load_test.wait()
    load_emb.wait()

    order = (2, 1, 3, 0)
    low, high = pl.ds(0, half), pl.ds(half, half)
    core_copies, relays, arrivals = [], [], []

    def hand_on(step):
        core_copies[step].wait()
        mine = part.at[step, k]
        mine[...] = mine[...] + by_core[step]
        if order[step] == 2:
            relays.append(send(mine.at[low], relay.at[0], relay_sems, 0, right))
            relays.append(send(mine.at[high], relay.at[1], relay_sems, 1, left))
        elif order[step] == 1:
            arrivals.append(send(mine.at[high], by_x.at[0, high], x_sems, 0, right))
            relays[0].wait()
            mine[low, :] = mine[low, :] + relay[0]
            arrivals.append(send(mine.at[low], by_x.at[0, low], x_sems, 1, right))
        elif order[step] == 3:
            arrivals.append(send(mine.at[low], by_x.at[1, low], x_sems, 2, left))
            relays[1].wait()
            mine[high, :] = mine[high, :] + relay[1]
            arrivals.append(send(mine.at[high], by_x.at[1, high], x_sems, 3, left))

    for step, d in enumerate(order):
        target = (x + d) % XS

        @pl.loop(0, 2)
        def _(half):
            first = pl.multiple_of((target * 2 + half) * share, share)
            part[step, half] = dot(emb[pl.ds(first, share), :], test[...], 1, 0)

        if step == 0:
            pl.semaphore_wait(barrier, count)
        core_copies.append(send(part.at[step, 1 - k], by_core.at[step], core_sems, step, sibling))
        if step:
            hand_on(step - 1)
    hand_on(3)

    @pl.loop(0, XS)
    def _(source):
        rows = emb[pl.ds(pl.multiple_of(source * rows_x, rows_x), rows_x), :]
        emb_t[source] = rows.T

    proj_a[...] = jnp.zeros_like(proj_a)
    proj_b[...] = jnp.zeros_like(proj_b)
    wait(arrivals)
    own = part[3, k] + (by_x[0] + by_x[1])
    share_ref[...] = own
    stores = [pltpu.make_async_copy(share_ref, share_out, store_sems.at[0])]
    stores[0].start()
    own_rows = pl.ds(pl.multiple_of(me * share, share), share)
    slab_a[own_rows, :] = own[:, :cut]
    slab_b[own_rows, :] = own[:, cut:]

    def piece(slab, source, first, rows):
        return slab.at[pl.ds(pl.multiple_of(source * share, share) + first, rows)]

    def same(slab, sems, slot, source, first, rows, to):
        ref = piece(slab, source, first, rows)
        return send(ref, ref, sems, slot, to)

    def gather_slab(slab, x_sems, core_sems):
        copies = [
            same(slab, x_sems, 0, me, 0, half, right),
            same(slab, x_sems, 1, me, half, half, left),
            same(slab, x_sems, 2, me, half, half, right),
            same(slab, x_sems, 3, me, 0, half, left),
        ]
        across = [same(slab, core_sems, 0, me, 0, share, sibling)]
        before, after, far = [((x + d) % XS) * 2 + k for d in (3, 1, 2)]
        yield across
        copies[0].wait()
        copies.append(same(slab, x_sems, 4, before, 0, half, right))
        copies[1].wait()
        copies.append(same(slab, x_sems, 5, after, half, half, left))
        yield
        copies[2].wait()
        across.append(same(slab, core_sems, 1, before, 0, share, sibling))
        copies[3].wait()
        across.append(same(slab, core_sems, 2, after, 0, share, sibling))
        yield
        copies[4].wait()
        copies[5].wait()
        across.append(same(slab, core_sems, 3, far, 0, share, sibling))
        yield

    def project(across, slab, into, step):
        across[step].wait()
        source = (x + (0, 3, 1, 2)[step]) % XS
        rows = slab[pl.ds(pl.multiple_of(source * rows_x, rows_x), rows_x), :]
        into[...] = into[...] + dot(emb_t[source], rows, 1, 0)

    gather_a = gather_slab(slab_a, gxa_sems, gka_sems)
    across_a = next(gather_a)
    slots_of(share_ref, gram_part)
    gram_sum = sum_gram(
        here, gram_part, (sum_y, sum_z), (g_k, g_y, g_z, g_x),
        dict(k=gs_k, y=gs_y, z=gs_z, x=gs_x, gz=gs_gz, gy=gs_gy, gk=gs_gk), gram_out,
    )
    next(gram_sum, None)
    next(gram_sum, None)
    next(gather_a)
    gather_b = gather_slab(slab_b, gxb_sems, gkb_sems)
    across_b = next(gather_b)
    project(across_a, slab_a, proj_a, 0)
    next(gather_a)
    next(gather_a)
    project(across_a, slab_a, proj_a, 1)
    next(gram_sum, None)
    next(gather_b)
    project(across_a, slab_a, proj_a, 2)
    project(across_a, slab_a, proj_a, 3)
    sum_a = sum_rows(here, "yz", proj_a, a_sum, (a_in0, a_in1), (a_s0, a_s1, a_s2, a_s3), a_out)
    next(sum_a, None)
    project(across_b, slab_b, proj_b, 0)
    next(gather_b)
    next(gram_sum, None)
    next(gather_b)
    project(across_b, slab_b, proj_b, 1)
    project(across_b, slab_b, proj_b, 2)
    next(gram_sum, None)
    project(across_b, slab_b, proj_b, 3)
    middle = slab_b.shape[1] // 2
    sum_c = sum_rows(
        here, "yz", proj_b.at[:, :middle], c_sum, (c_in0, c_in1), (c_s0, c_s1, c_s2, c_s3), c_out
    )
    sum_b = sum_rows(
        here, "zy", proj_b.at[:, middle:], b_sum, (b_in0, b_in1), (b_s0, b_s1, b_s2, b_s3), b_out
    )
    next(sum_b, None)
    next(sum_c, None)
    next(gram_sum, None)
    next(sum_a, None)
    next(sum_c, None)
    next(gram_sum, None)
    next(sum_b, None)
    next(gram_sum, None)

    load_gram(gram_out, gram, row_scale)
    step_a, step_b, step_c = [functools.partial(next, item, None) for item in (sum_a, sum_b, sum_c)]
    hooks = {
        0: {4: step_a, 9: step_b, 10: step_c},
        1: {6: step_b, 15: step_a},
        2: {6: step_c},
    }
    for _ in factor_steps(gram, inverse_ref, hooks=hooks):
        pass
    stores.append(pltpu.make_async_copy(inverse_ref, inverse_out, store_sems.at[1]))
    stores[1].start()
    step_a()
    step_b()
    step_c()
    far = cut + middle
    dual_ref[:, :cut] = dot(a_out[...], inverse_ref[:cut, :cut], 1, 1)
    dual_ref[:, cut:] = (
        dot(a_out[...], inverse_ref[cut:, :cut], 1, 1)
        + dot(c_out[...], inverse_ref[cut:, cut:far], 1, 1)
        + dot(b_out[...], inverse_ref[cut:, far:], 1, 1)
    )

    stores.append(pltpu.make_async_copy(dual_ref, dual_out, store_sems.at[2]))
    stores[2].start()

    for i in range(dual_cols.shape[0]):
        dual_cols[i] = dual_ref[:, i * BLOCK : (i + 1) * BLOCK]
    for i in range(4):
        row, col = block_of(4 * y + i)
        dual_part[pl.ds(i * BLOCK, BLOCK), :] = dot(
            dual_cols[jnp.maximum(row, col)], dual_cols[jnp.minimum(row, col)], 0, 0
        )
    mine = pl.ds(pl.multiple_of(k * 256, 256), 256)
    theirs = pl.ds(pl.multiple_of((1 - k) * 256, 256), 256)
    send(dual_part.at[theirs], d_k, ds_k, 0, sibling).wait()
    d_sum[...] = dual_part[mine, :] + d_k[...]
    wait(scatter("x", here, d_sum, 64, d_x, ds_x))
    done = pl.ds(pl.multiple_of(y * 512 + k * 256 + x * 64, 64), 64)
    slots_ref[done, :] = total(d_sum[pl.ds(pl.multiple_of(x * 64, 64), 64), :], d_x)
    wait(
        [
            send(slots_ref.at[done], slots_ref.at[done], ds_gxy, i, peer)
            for i, peer in enumerate(plane(here))
        ]
    )
    copies = []
    for i in range(YS):
        both = pl.ds(pl.multiple_of(i * 512 + k * 256, 256), 256)
        copies.append(send(slots_ref.at[both], slots_ref.at[both], ds_gk, i, sibling))
    wait(copies)
    wait(stores)


def block_of(slot):
    return slot % 5, (slot % 5 + slot // 5) % 5


def dma(*shape):
    return pltpu.SemaphoreType.DMA(shape)


def vmem(*shape):
    return pltpu.VMEM(shape, jnp.float32)


def pair(n):
    return dma(2, n)


def sketch_step(embedding, test_matrix, row_scale):
    rows, width = embedding.shape
    rank = test_matrix.shape[1]
    share = rows // 8
    a, b = 384, rank - 384
    f32 = lambda *shape: jax.ShapeDtypeStruct(shape, jnp.float32)
    scratch = [vmem(share, rank), vmem(rank, rank), vmem(width, rank), dma(3)]
    scratch += [vmem(rows, width), vmem(XS, width, rows // XS), vmem(width, rank), dma(2)]
    scratch += [vmem(4, 2, share, rank), vmem(4, share, rank), vmem(2, share // 2, rank)]
    scratch += [vmem(2, share, rank), pair(4), pair(2), pair(4)]
    scratch += [vmem(rows, a), vmem(rows, b), pair(6), pair(6), pair(4), pair(4)]
    scratch += [vmem(width, a), vmem(width, b)]
    scratch += [vmem(width // 4, a), vmem(3, width // 4, a), vmem(7, width // 32, a), vmem(width, a)]
    scratch += [pair(3), pair(7), pair(7), pair(3)]
    c = b // 2
    scratch += [vmem(width // 8, c), vmem(7, width // 8, c), vmem(3, width // 32, c), vmem(width, c)]
    scratch += [pair(7), pair(3), pair(3), pair(7)]
    scratch += [vmem(width // 4, c), vmem(3, width // 4, c), vmem(7, width // 32, c), vmem(width, c)]
    scratch += [pair(3), pair(7), pair(7), pair(3)]
    scratch += [vmem(2, 1024, 128), vmem(2, 1024, 128), vmem(256, 128), vmem(32, 128)]
    scratch += [vmem(1024, 128), vmem(3, 256, 128), vmem(7, 32, 128), vmem(4, 32, 128)]
    scratch += [pair(1), pair(3), pair(7), pair(3), pair(7), pair(3), pair(1)]
    scratch += [vmem(rank, rank), vmem(rank // BLOCK, width, BLOCK), vmem(512, 128)]
    scratch += [vmem(256, 128), vmem(256, 128), vmem(3, 64, 128)]
    scratch += [pair(1), pair(3), pair(YS * XS - 1), pair(YS)]
    return pl.pallas_call(
        functools.partial(sketch_kernel, row_scale),
        out_shape=(f32(share, rank), f32(rank, rank), f32(width, rank), f32(2048, 128)),
        in_specs=[pl.BlockSpec(memory_space=pl.ANY)] * 2,
        out_specs=[pl.BlockSpec(memory_space=pl.ANY)] * 3 + [pl.BlockSpec(memory_space=pltpu.VMEM)],
        scratch_shapes=scratch,
        name="sketch_step",
        compiler_params=pltpu.CompilerParams(
            collective_id=0, has_side_effects=True, vmem_limit_bytes=VMEM_LIMIT
        ),
    )(embedding, test_matrix)


def load_gram(slots_ref, gram, scale):
    for i in range(5):
        for j in range(i + 1):
            slot = i * (i + 1) // 2 + j
            block = slots_ref[slot // 8, pl.ds((slot % 8) * BLOCK, BLOCK), :]
            gram[pl.ds(i * BLOCK, BLOCK), pl.ds(j * BLOCK, BLOCK)] = block * scale


def factor_steps(gram, inverse=None, mats=(), work=(), hooks={}):
    rank = gram.shape[0]
    work = list(work)
    ahead = {}
    if inverse is not None:
        inverse[...] = jnp.zeros_like(inverse)

    def update(rows, cols, lo):
        source = slice(lo, lo + BLOCK)
        gram[rows, cols] = gram[rows, cols] - dot(gram[rows, source], gram[cols, source], 1, 1)

    def solve(rows, lo, block):
        gram[rows, lo : lo + BLOCK] = dot(gram[rows, lo : lo + BLOCK], block, 1, 1)

    def apply(mat, lo, block):
        mat[:, lo : lo + BLOCK] = dot(mat[:, lo : lo + BLOCK], block, 1, 1)

    def reduce(mat, cols, lo):
        source = slice(lo, lo + BLOCK)
        mat[:, cols] = mat[:, cols] - dot(mat[:, source], gram[cols, source], 1, 1)

    def finish(lo, block):
        inverse[lo : lo + BLOCK, :lo] = -dot(block, ahead[lo], 1, 0)

    def prepare(lo):
        ahead[lo] = dot(gram[lo : lo + BLOCK, :lo], inverse[:lo, :lo], 1, 0)

    call = functools.partial
    for lo in range(0, rank, BLOCK):
        hi = lo + BLOCK
        tiles = [gram[lo + TILE * i : lo + TILE * (i + 1), lo:hi] for i in range(TILES)]
        block = invert_factor(tiles, work, hooks.get(lo // BLOCK, {}))
        work = []
        following = [slice(i, i + BLOCK) for i in range(hi, rank, BLOCK)]
        if following:
            solve(following[0], lo, block)
            update(following[0], following[0], lo)
        if following[1:]:
            work.append(call(solve, slice(hi + BLOCK, rank), lo, block))
            work.append(call(update, slice(hi + BLOCK, rank), following[0], lo))
            work += [call(update, slice(cols.start, rank), cols, lo) for cols in following[1:]]
        if inverse is not None:
            inverse[lo:hi, lo:hi] = block
            if lo:
                work.append(call(finish, lo, block))
            if following:
                work.append(call(prepare, hi))
        for mat in mats:
            work.append(call(apply, mat, lo, block))
            work += [call(reduce, mat, cols, lo) for cols in following]
        if not following:
            for item in work:
                item()
        yield


def last_kernel(
    scale, slots_ref, dual_hbm, share_hbm, inverse_hbm, white_ref, basis_ref, gram, share_ref, inverse_ref, sems
):
    loads = [
        pltpu.make_async_copy(source, into, sems.at[i])
        for i, (source, into) in enumerate(
            ((share_hbm, share_ref), (inverse_hbm, inverse_ref), (dual_hbm, basis_ref))
        )
    ]
    for load in loads:
        load.start()
    for slot in range(15):
        row, col = block_of(slot)
        row, col = max(row, col), min(row, col)
        gram[row * BLOCK : (row + 1) * BLOCK, col * BLOCK : (col + 1) * BLOCK] = (
            slots_ref[slot * BLOCK : (slot + 1) * BLOCK, :] * scale
        )

    def whiten(cols):
        white_ref[:, cols] = dot(share_ref[...], inverse_ref[cols, :], 1, 1)

    work = [lambda: None] * 6 + [functools.partial(wait, loads)]
    work += [functools.partial(whiten, slice(i, i + BLOCK)) for i in range(0, gram.shape[0], BLOCK)]
    for _ in factor_steps(gram, mats=(basis_ref,), work=work):
        pass


def body(embedding, test_matrix):
    rows_local, width_local = embedding.shape
    total_rows = rows_local * lax.axis_size("rows")
    total_width = width_local * lax.axis_size("cols")
    rank = test_matrix.shape[1]
    f32 = lambda *shape: jax.ShapeDtypeStruct(shape, jnp.float32)
    share, inverse, dual, slots = sketch_step(embedding, test_matrix, 1.0 / total_rows)
    return pl.pallas_call(
        functools.partial(last_kernel, 1.0 / total_width),
        out_shape=(f32(*share.shape), f32(width_local, rank)),
        in_specs=[pl.BlockSpec(memory_space=pltpu.VMEM)] + [pl.BlockSpec(memory_space=pl.ANY)] * 3,
        scratch_shapes=[vmem(rank, rank), vmem(*share.shape), vmem(rank, rank), dma(3)],
        name="whiten_both",
        compiler_params=pltpu.CompilerParams(vmem_limit_bytes=VMEM_LIMIT),
    )(slots, dual, share, inverse)


def solution(mesh):
    placed = (P("rows", "cols"), P("cols", None))
    return jax.shard_map(
        body,
        mesh=mesh,
        in_specs=placed,
        out_specs=(P(("rows", "cols"), None), P("cols", None)),
        check_vma=False,
    )
```
